128 devices in a mesh: group: 16 (over y, z), tensor: 8 (over x, core).
Axes of the slice: x: 4, y: 4, z: 4, core: 2. Of those that a mesh axis runs over, the one named last changes fastest.
Arguments:
- query: bfloat16 [4096, 8192], P('group', 'tensor'), may hold values from -4.5 to 4.5
- resp_key: bfloat16 [4096, 1024], P('group', 'tensor'), may hold values from -4.5 to 4.5
- resp_value: bfloat16 [4096, 1024], P('group', 'tensor'), may hold values from -4.5 to 4.5
- prefix_key: bfloat16 [4096, 1024], P('group', 'tensor'), may hold values from -4.5 to 4.5
- prefix_value: bfloat16 [4096, 1024], P('group', 'tensor'), may hold values from -4.5 to 4.5
- readout: bfloat16 [4096, 8192], P('group', 'tensor'), may hold values from -0.0625 to 0.0625
- logit_base: float32 [4096], P('group'), may hold values from -3 to 3
- ref_logprob: float32 [4096], P('group'), may hold values from -3 to -0.1
- advantage: float32 [16], P('group'), may hold values from -3 to 3
- resp_length: int32 [16], P('group'), may hold values from 64 to 256, as said below
- token_count: int32 [1], replicated, may hold values from 2048 to 8191
Outputs:
- loss: float32 [1], replicated
- grad_query: bfloat16 [4096, 8192], P('group', 'tensor')
- grad_resp_key: bfloat16 [4096, 1024], P('group', 'tensor')
- grad_resp_value: bfloat16 [4096, 1024], P('group', 'tensor')
- grad_prefix_key: bfloat16 [4096, 1024], P('group', 'tensor')
- grad_prefix_value: bfloat16 [4096, 1024], P('group', 'tensor')
The draws below stay inside these ranges and needn't reach their ends.
Inputs may be any that keep to these rules, and one draw needn't show every extreme that they name: `resp_length`: one response has exactly 256 tokens.
All inputs are finite; a program needn't handle non-finite values.
Results may differ from the reference program's by a relative error of at most 0.022.
Values may be sent and summed in bfloat16 or wider, within the bound.
A program may use at most 128 MiB of HBM per device.

```python
import jax
import jax.numpy as jnp
from jax import lax

HEADS = 64
KVH = 8
DH = 128
RESP = 256
RTOK = 4096
PREFIX = 4096
N_GROUP = 16


def draw_prefix_key(key, part):
    key = jax.random.fold_in(key, 11)
    drawn = jnp.clip(jax.random.normal(key, (PREFIX, KVH * DH), jnp.float32), -4.5, 4.5)
    return drawn.astype(jnp.bfloat16)


def draw_query(key, part):
    key = jax.random.fold_in(key, 12)
    drawn = jnp.clip(jax.random.normal(key, (RTOK, HEADS * DH), jnp.float32), -4.5, 4.5)
    return drawn.astype(jnp.bfloat16)


def draw_resp_length(key, part):
    key = jax.random.fold_in(key, 13)
    first_key, second_key = jax.random.split(key)
    members = RTOK // RESP
    drawn = jax.random.randint(first_key, (members,), RESP // 4, RESP + 1)
    longest = jax.random.randint(second_key, (), 0, members)
    return jnp.where(jnp.arange(members) == longest, RESP, drawn).astype(jnp.int32)


def block_scale(key, shape, cuts, least, high):
    level = 1.0
    for axis_at, shards_of in cuts:
        steps = jax.random.uniform(jax.random.fold_in(jax.random.fold_in(key, 6), axis_at), (shards_of,), jnp.float32, least / len(cuts), high / len(cuts))
        level = level * jnp.repeat(jnp.exp(steps), shape[axis_at] // shards_of).reshape((-1,) + (1,) * (len(shape) - 1 - axis_at))
    return level


def bell_draw(stream_key, dims, width, most, cuts=(), kind=jnp.bfloat16):
    loudness = block_scale(stream_key, dims, cuts, -0.22, 0.18) if cuts else 1.0
    array = jax.random.normal(stream_key, dims, jnp.float32) * width * loudness
    return jnp.minimum(jnp.maximum(array, -most), most).astype(kind)


def setup_inputs(seed: int = 0) -> dict:
    streams_of = jax.random.split(jax.random.key(seed), 12)
    query = draw_query(jax.random.fold_in(streams_of[11], 71), 0)
    resp_key = bell_draw(streams_of[1], (RTOK, KVH * DH), 1.0, 4.5, ((0, 16), (1, 8)))
    resp_value = bell_draw(streams_of[2], (RTOK, KVH * DH), 1.0, 4.5, ((0, 16), (1, 8)))
    prefix_key = draw_prefix_key(jax.random.fold_in(streams_of[11], 71), 0)
    prefix_value = bell_draw(streams_of[4], (PREFIX, KVH * DH), 1.0, 4.5, ((0, 16), (1, 8)))
    readout = bell_draw(streams_of[5], (RTOK, HEADS * DH), (HEADS * DH) ** -0.5, 0.0625, ((0, 16), (1, 8)))
    logit_base = bell_draw(streams_of[6], (RTOK,), 1.0, 3.0, ((0, 16),), jnp.float32)
    ref_logprob = jnp.clip(-3.0 + 2.9 * jax.random.uniform(streams_of[7], (RTOK,), jnp.float32) ** block_scale(streams_of[7], (RTOK,), ((0, 16),), -0.2, 0.2), -3.0, -0.1)
    advantage = bell_draw(streams_of[8], (N_GROUP,), 1.0, 3.0, ((0, 16),), jnp.float32)
    resp_length = draw_resp_length(jax.random.fold_in(streams_of[11], 71), 0)
    token_count = jax.random.randint(streams_of[10], (1,), RTOK // 2, 2 * RTOK).astype(jnp.int32)
    return dict(query=query, resp_key=resp_key, resp_value=resp_value, prefix_key=prefix_key, prefix_value=prefix_value, readout=readout, logit_base=logit_base, ref_logprob=ref_logprob, advantage=advantage, resp_length=resp_length, token_count=token_count)


score_floor = -1.0e30
grad_boost = 64.0


def judge(logit_value, ref_rows, is_valid, advantage_value, token_total, grad_factor):
    logprob = jax.nn.log_sigmoid(logit_value)
    log_gap = ref_rows - logprob
    token_terms = jnp.where(is_valid, jnp.exp(log_gap) - log_gap - 1.0 - advantage_value * logprob, 0.0)
    d_logit = jnp.where(is_valid, (1.0 - jnp.exp(log_gap) - advantage_value) * jax.nn.sigmoid(-logit_value), 0.0) * (grad_factor / token_total)
    return d_logit, token_terms


def rounded(values):
    return lax.optimization_barrier(values.astype(jnp.bfloat16)).astype(jnp.float32)


def reference(query, resp_key, resp_value, prefix_key, prefix_value, readout, logit_base, ref_logprob, advantage, resp_length, token_count):
    groups = HEADS // KVH
    score_scale = DH ** -0.5
    grad_factor = grad_boost * RTOK
    prefix_keys = prefix_key.astype(jnp.float32).reshape(PREFIX, KVH, DH)
    prefix_values = prefix_value.astype(jnp.float32).reshape(PREFIX, KVH, DH)
    causal = jnp.arange(RESP)[:, None] >= jnp.arange(RESP)[None, :]
    allowed = jnp.concatenate([jnp.ones((RESP, PREFIX), dtype=bool), causal], axis=1)
    token_total = token_count[0].astype(jnp.float32)
    positions = jnp.arange(RESP)

    def respond(carry, resp_index):
        grad_pk, grad_pv, loss_sum = carry
        first_row = (resp_index * RESP).astype(jnp.int32)

        def pick_rows(source):
            return lax.dynamic_slice_in_dim(source, first_row, RESP, 0)

        queries = pick_rows(query).astype(jnp.float32).reshape(RESP, KVH, groups, DH)
        all_keys = jnp.concatenate([prefix_keys, pick_rows(resp_key).astype(jnp.float32).reshape(RESP, KVH, DH)], 0)
        all_values = jnp.concatenate([prefix_values, pick_rows(resp_value).astype(jnp.float32).reshape(RESP, KVH, DH)], 0)
        scores = jnp.einsum("rkgd,skd->kgrs", queries, all_keys) * score_scale
        scores = jnp.where(allowed, scores, score_floor)
        row_max = scores.max(-1, keepdims=True)
        exponent = jnp.exp(scores - row_max)
        row_sum = exponent.sum(-1, keepdims=True)
        attended = jnp.einsum("kgrs,skd->kgrd", rounded(exponent), all_values) / row_sum
        weight_out = pick_rows(readout).astype(jnp.float32).reshape(RESP, KVH, groups, DH)
        logit_value = pick_rows(logit_base) + jnp.einsum("kgrd,rkgd->r", attended, weight_out)
        is_valid = positions < resp_length[resp_index]
        d_logit, token_terms = judge(logit_value, pick_rows(ref_logprob), is_valid, advantage[resp_index], token_total, grad_factor)
        grad_out = rounded(d_logit[:, None] * pick_rows(readout).astype(jnp.float32))
        grad_out = grad_out.reshape(RESP, KVH, groups, DH).transpose(1, 2, 0, 3)
        row_dot = jnp.sum(grad_out * attended, -1, keepdims=True)
        log_total = row_max + jnp.log(row_sum)
        weights_full = jnp.exp(scores - log_total)
        grad_values = jnp.einsum("kgrs,kgrd->skd", rounded(weights_full), grad_out)
        d_probs = jnp.einsum("kgrd,skd->kgrs", grad_out, all_values)
        d_scores = rounded(weights_full * (d_probs - row_dot))
        grad_q = jnp.einsum("kgrs,skd->rkgd", d_scores, all_keys) * score_scale
        grad_keys = jnp.einsum("kgrs,rkgd->skd", d_scores, queries) * score_scale
        new_carry = (grad_pk + grad_keys[:PREFIX], grad_pv + grad_values[:PREFIX], loss_sum + jnp.sum(token_terms))
        outputs = (grad_q.reshape(RESP, HEADS * DH).astype(jnp.bfloat16),
                   grad_keys[PREFIX:].reshape(RESP, KVH * DH).astype(jnp.bfloat16),
                   grad_values[PREFIX:].reshape(RESP, KVH * DH).astype(jnp.bfloat16))
        return new_carry, outputs

    start_carry = (jnp.zeros((PREFIX, KVH, DH), jnp.float32), jnp.zeros((PREFIX, KVH, DH), jnp.float32), jnp.zeros((), jnp.float32))
    final_carry, stacked = lax.scan(respond, start_carry, jnp.arange(RTOK // RESP, dtype=jnp.int32))
    grad_pk, grad_pv, loss_sum = final_carry
    loss = (loss_sum / token_total).reshape(1)
    return (loss, stacked[0].reshape(RTOK, HEADS * DH), stacked[1].reshape(RTOK, KVH * DH), stacked[2].reshape(RTOK, KVH * DH),
            grad_pk.reshape(PREFIX, KVH * DH).astype(jnp.bfloat16), grad_pv.reshape(PREFIX, KVH * DH).astype(jnp.bfloat16))
```

```python
import functools

import jax
import jax.numpy as jnp
from jax import lax
from jax.experimental import pallas as pl
from jax.experimental.pallas import tpu as pltpu
from jax.sharding import PartitionSpec as P

MESH = pl.DeviceIdType.MESH
bf16 = jnp.bfloat16
f32 = jnp.float32
NT = (((1,), (1,)), ((), ()))

DH = 128
TOK = 256
HPD = 8
ROWS = TOK * HPD
KEYS = 4096 + TOK
SIDE = 4
HALF = 128
STEPS = (1, 3, 2)
OWN_A, OWN_B, NEAR, FAR = 256, 384, 512, 1280
OWN, GROUP = 512, 768
LAST = 5
SCORE_SCALE = DH**-0.5
TO_LOG2 = SCORE_SCALE * 1.4426950408889634
SCORE_FLOOR = -1e30
GRAD_FACTOR = 64.0 * 4096.0


def block_at(b):
    if isinstance(b, int):
        return (0, OWN) if b == 0 else (OWN + GROUP * (b - 1), GROUP)
    return pl.multiple_of(OWN + GROUP * (b - 1), 256), GROUP


def fold_rows(x):
    return jnp.sum(x.reshape(-1, 8, x.shape[-1]), 0)


def cols(h, width):
    return slice(h * width, (h + 1) * width)


def score_stage(r, h, b, buf, first):
    row0, size = block_at(b)
    s = (
        lax.dot_general(
            r["kv"][pl.ds(row0, size), :DH],
            r["q"][:, cols(h, DH)],
            NT,
            preferred_element_type=f32,
        )
        * TO_LOG2
    )
    if first:
        key_at = lax.broadcasted_iota(jnp.int32, (TOK, TOK), 0)
        query_at = lax.broadcasted_iota(jnp.int32, (TOK, TOK), 1)
        s = jnp.concatenate([jnp.where(key_at <= query_at, s[:TOK], SCORE_FLOOR), s[TOK:]], 0)
    buf[:size, :] = s
    top = jnp.ceil(jnp.max(jnp.max(s.reshape(-1, 8, TOK), 0), 0, keepdims=True))
    if not first:
        top = jnp.maximum(top, r["top"][b - 1, h : h + 1, :])
    r["top"][b, h : h + 1, :] = top


def weight_stage(r, h, b, buf, first):
    row0, size = block_at(b)
    at = cols(h, TOK)
    along = lax.dot_general(
        r["kv"][pl.ds(row0, size), DH:],
        r["ro"][:, cols(h, DH)],
        NT,
        preferred_element_type=f32,
    )
    top = r["top"][b, h : h + 1, :]
    e = jnp.exp2(buf[:size, :] - top)
    r["e"][pl.ds(row0, size), at] = e.astype(bf16)
    r["along"][pl.ds(row0, size), at] = along
    if first:
        r["l"][:, at] = fold_rows(e)
        r["dot"][:, at] = fold_rows(e * along)
    else:
        shrink = jnp.exp2(r["top"][b - 1, h : h + 1, :] - top)
        r["l"][:, at] = r["l"][:, at] * shrink + fold_rows(e)
        r["dot"][:, at] = r["dot"][:, at] * shrink + fold_rows(e * along)


def forward_block(r, b, first=False):
    bufs = (r["s0"], r["s1"])
    score_stage(r, 0, b, bufs[0], first)
    for h in range(HPD):
        if h + 1 < HPD:
            score_stage(r, h + 1, b, bufs[(h + 1) % 2], first)
        weight_stage(r, h, b, bufs[h % 2], first)


def query_block(r, b, first=False):
    row0, size = block_at(b)
    rows = pl.ds(row0, size)
    r["kt"][:, :size] = jnp.transpose(r["kv"][rows, :DH].astype(f32)).astype(bf16)
    for h in range(HPD):
        at = cols(h, TOK)
        x = r["e"][rows, at].astype(f32) * (r["along"][rows, at] - r["mean"][h : h + 1, :])
        r["along"][rows, at] = x
        d = jnp.dot(r["kt"][:, :size], x.astype(bf16), preferred_element_type=f32)
        d = d * jnp.exp2(r["top"][b, h : h + 1, :] - r["top"][LAST, h : h + 1, :])
        r["dq"][:, at] = d if first else r["dq"][:, at] + d


def grads_block(r, b):
    row0, size = block_at(b)
    rows = pl.ds(row0, size)
    c = jnp.transpose(r["c"][...] * jnp.exp2(r["top"][b] - r["top"][LAST]))
    ck = c * SCORE_SCALE
    for h in range(HPD):
        at = cols(h, TOK)
        r["wv"][at, :] = (r["ro"][:, cols(h, DH)].astype(f32) * c[:, h : h + 1]).astype(bf16)
        r["wq"][at, :] = (r["q"][:, cols(h, DH)].astype(f32) * ck[:, h : h + 1]).astype(bf16)
    r["kv"][rows, DH:] = jnp.dot(
        r["e"][rows, :], r["wv"][...], preferred_element_type=f32
    ).astype(bf16)
    r["kv"][rows, :DH] = jnp.dot(
        r["along"][rows, :].astype(bf16), r["wq"][...], preferred_element_type=f32
    ).astype(bf16)


def judge(logit, ref_rows, is_valid, advantage, token_total):
    logprob = jnp.minimum(logit, 0.0) - jnp.log1p(jnp.exp(-jnp.abs(logit)))
    gap = ref_rows - logprob
    ratio = jnp.exp(gap)
    terms = jnp.where(is_valid, ratio - gap - 1.0 - advantage * logprob, 0.0)
    d_logit = jnp.where(
        is_valid, (1.0 - ratio - advantage) * jax.nn.sigmoid(-logit), 0.0
    ) * (GRAD_FACTOR / token_total)
    return d_logit, terms


NAMES = (
    ["e", "along", "kv", "q", "ro", "s0", "s1", "kt", "dq", "wv", "wq", "top", "l", "dot"]
    + ["mean", "c", "got", "got2", "part", "loss_z", "loss_y", "lb", "rf", "load_sem"]
    + ["ag_send", "ag_recv", "part_send", "part_recv", "rs_send", "rs_recv"]
    + ["rs2_send", "rs2_recv", "lz_send", "lz_recv", "ly_send", "ly_recv"]
)


def scratch():
    vm, dma = pltpu.VMEM, pltpu.SemaphoreType.DMA
    return [
        vm((KEYS, ROWS), bf16),
        vm((KEYS, ROWS), f32),
        vm((KEYS, 2 * DH), bf16),
        vm((TOK, HPD * DH), bf16),
        vm((TOK, HPD * DH), bf16),
        vm((GROUP, TOK), f32),
        vm((GROUP, TOK), f32),
        vm((DH, GROUP), bf16),
        vm((DH, ROWS), f32),
        vm((ROWS, DH), bf16),
        vm((ROWS, DH), bf16),
        vm((LAST + 1, HPD, TOK), f32),
        vm((8, ROWS), f32),
        vm((8, ROWS), f32),
        vm((HPD, TOK), f32),
        vm((HPD, TOK), f32),
        vm((4, GROUP, 2 * DH), bf16),
        vm((2, 3, HALF, 2 * DH), bf16),
        vm((8, 8, TOK), f32),
        vm((SIDE, 8, 128), f32),
        vm((SIDE, 8, 128), f32),
        vm((1, TOK), f32),
        vm((1, TOK), f32),
        dma((16,)),
        dma((30,)),
        dma((30,)),
        dma((8,)),
        dma((8,)),
        dma((24,)),
        dma((24,)),
        dma((6,)),
        dma((6,)),
        dma((3,)),
        dma((SIDE,)),
        dma((3,)),
        dma((SIDE,)),
    ]


def kernel(*refs):
    (q, ro, rk, rv, pk, pv, lb, rf, adv, rlen, count) = refs[:11]
    (loss, gq, grk, grv, gpk, gpv) = refs[11:17]
    r = dict(zip(NAMES, refs[17:]))
    kv = r["kv"]

    g, t = lax.axis_index("group"), lax.axis_index("tensor")
    y, z = g // SIDE, g % SIDE

    def along_z(step):
        return (y * SIDE + (z + step) % SIDE, t)

    def along_y(step):
        return (((y + step) % SIDE) * SIDE + z, t)

    def in_tensor(step):
        return (g, (t + step) % 8)

    moves = [
        (pk.at[:HALF], kv.at[OWN_A : OWN_A + HALF, :DH]),
        (pk.at[HALF:], kv.at[OWN_B : OWN_B + HALF, :DH]),
        (pv.at[:HALF], kv.at[OWN_A : OWN_A + HALF, DH:]),
        (pv.at[HALF:], kv.at[OWN_B : OWN_B + HALF, DH:]),
        (rk, kv.at[:TOK, :DH]),
        (rv, kv.at[:TOK, DH:]),
        (q, r["q"]),
        (ro, r["ro"]),
        (lb, r["lb"]),
        (rf, r["rf"]),
    ]
    loads = [
        pltpu.make_async_copy(src, dst, r["load_sem"].at[i]) for i, (src, dst) in enumerate(moves)
    ]
    for load in loads:
        load.start()

    barrier = pltpu.get_barrier_semaphore()
    peers = (
        [along_z(d) for d in STEPS]
        + [along_y(d) for d in STEPS]
        + [in_tensor(d) for d in range(1, 8)]
    )
    for peer in peers:
        pl.semaphore_signal(barrier, inc=1, device_id=peer, device_id_type=MESH)
    for load in loads[:4]:
        load.wait()
    pl.semaphore_wait(barrier, len(peers))

    def part_of_code(body):
        pl.when(t >= 0)(body)

    def remote(src, dst, send_sem, recv_sem, peer):
        return pltpu.make_async_remote_copy(
            src_ref=src,
            dst_ref=dst,
            send_sem=send_sem,
            recv_sem=recv_sem,
            device_id=peer,
            device_id_type=MESH,
        )

    def gather_copy(slot, src_row, dst_row, peer):
        return remote(
            kv.at[src_row : src_row + HALF],
            kv.at[dst_row : dst_row + HALF],
            r["ag_send"].at[slot],
            r["ag_recv"].at[slot],
            peer,
        )

    near = [gather_copy(j, OWN_A, NEAR + HALF * j, along_z(-STEPS[j])) for j in range(3)]
    near += [
        gather_copy(3 + j, OWN_B, NEAR + 384 + HALF * j, along_y(-STEPS[j])) for j in range(3)
    ]
    far = []
    for i in range(4):
        src_a = OWN_A if i == 0 else NEAR + HALF * (i - 1)
        src_b = OWN_B if i == 0 else NEAR + 384 + HALF * (i - 1)
        dst = FAR + GROUP * i
        far.append(
            [gather_copy(6 + 6 * i + k, src_a, dst + HALF * k, along_y(-STEPS[k])) for k in range(3)]
            + [
                gather_copy(9 + 6 * i + k, src_b, dst + 384 + HALF * k, along_z(-STEPS[k]))
                for k in range(3)
            ]
        )
    for copy in near + far[0]:
        copy.start()
    for load in loads[4:]:
        load.wait()

    part_of_code(lambda: forward_block(r, 0, True))

    def forward_step(b, carry):
        @pl.when(b == 1)
        def _():
            for j in range(3):
                near[j].wait_recv()
                near[3 + j].wait_recv()
                for copy in far[j + 1]:
                    copy.start()

        for i in range(4):

            @pl.when(b == 2 + i)
            def _():
                for copy in far[i]:
                    copy.wait_recv()

        forward_block(r, b)
        return carry

    lax.fori_loop(1, LAST + 1, forward_step, 0)

    total = jnp.zeros((1, TOK), f32)
    sums = []
    for h in range(HPD):
        at = cols(h, TOK)
        row_sum = jnp.sum(r["l"][:, at], 0, keepdims=True)
        mean = jnp.sum(r["dot"][:, at], 0, keepdims=True) / row_sum
        r["mean"][h : h + 1, :] = mean
        r["c"][h : h + 1, :] = 1.0 / row_sum
        total = total + mean
    part = r["part"]
    part[t] = jnp.broadcast_to(total, (8, TOK))
    part_copies = [
        remote(
            part.at[t], part.at[t], r["part_send"].at[d], r["part_recv"].at[d], in_tensor(d)
        )
        for d in range(1, 8)
    ]
    for copy in part_copies:
        copy.start()

    part_of_code(lambda: query_block(r, 0, True))

    def query_step(n, carry):
        query_block(r, (3 * n + 1) // 2 + 1)
        return carry

    lax.fori_loop(0, 3, query_step, 0)

    for copy in part_copies:
        copy.wait()
    logit = r["lb"][...]
    for i in range(8):
        logit = logit + part[i, 0:1, :]
    token_total = count[0].astype(f32)
    is_valid = lax.broadcasted_iota(jnp.int32, (1, TOK), 1) < rlen[0]
    d_logit, terms = judge(logit, r["rf"][...], is_valid, adv[0], token_total)
    r["c"][...] = r["c"][...] * d_logit

    loss_z, loss_y = r["loss_z"], r["loss_y"]
    loss_z[z] = jnp.broadcast_to(jnp.sum(terms, axis=1, keepdims=True), (8, 128))
    lz = [
        remote(
            loss_z.at[z], loss_z.at[z], r["lz_send"].at[j], r["lz_recv"].at[STEPS[j]], along_z(STEPS[j])
        )
        for j in range(3)
    ]
    for copy in lz:
        copy.start()

    for copy in near:
        copy.wait_send()
    for group in far:
        for copy in group:
            copy.wait_send()

    def spread(i):
        row0 = FAR + GROUP * i
        return [
            remote(
                kv.at[pl.ds(row0 + HALF * n, HALF)],
                r["got"].at[i, pl.ds(HALF * n, HALF)],
                r["rs_send"].at[6 * i + n],
                r["rs_recv"].at[6 * i + n],
                along_y(STEPS[n]) if n < 3 else along_z(STEPS[n - 3]),
            )
            for n in range(6)
        ]

    second = []

    def second_stage(i):
        for copy in spread(i):
            copy.wait_recv()
        for side in range(2):
            row0 = NEAR + 384 * side + HALF * (i - 1)
            acc = kv[row0 : row0 + HALF, :].astype(f32)
            for k in range(3):
                at = 384 * side + HALF * k
                acc = acc + r["got"][i, at : at + HALF, :].astype(f32)
            kv[row0 : row0 + HALF, :] = acc.astype(bf16)
            slot = 2 * (i - 1) + side
            copy = remote(
                kv.at[row0 : row0 + HALF],
                r["got2"].at[side, i - 1],
                r["rs2_send"].at[slot],
                r["rs2_recv"].at[slot],
                along_y(STEPS[i - 1]) if side else along_z(STEPS[i - 1]),
            )
            copy.start()
            second.append(copy)

    def early_step(i, carry):
        grads_block(r, 2 + i)
        for copy in spread(i):
            copy.start()
        return carry

    def late_step(n, carry):
        i = 3 - 3 * n
        query_block(r, 2 + i)
        grads_block(r, 2 + i)
        for copy in spread(i):
            copy.start()
        return carry

    lax.fori_loop(1, 3, early_step, 0)
    part_of_code(lambda: grads_block(r, 1))

    for copy in lz:
        copy.wait()
    loss_y[y] = loss_z[0] + loss_z[1] + loss_z[2] + loss_z[3]
    ly = [
        remote(
            loss_y.at[y], loss_y.at[y], r["ly_send"].at[j], r["ly_recv"].at[STEPS[j]], along_y(STEPS[j])
        )
        for j in range(3)
    ]
    for copy in ly:
        copy.start()

    lax.fori_loop(0, 2, late_step, 0)
    second_stage(1)
    second_stage(2)
    part_of_code(lambda: grads_block(r, 0))
    stores = [
        pltpu.make_async_copy(kv.at[:TOK, :DH], grk, r["load_sem"].at[0]),
        pltpu.make_async_copy(kv.at[:TOK, DH:], grv, r["load_sem"].at[1]),
    ]
    for store in stores:
        store.start()
    second_stage(3)

    for h in range(HPD):
        d = r["dq"][:, cols(h, TOK)] * (r["c"][h : h + 1, :] * SCORE_SCALE)
        r["q"][:, cols(h, DH)] = jnp.transpose(d).astype(bf16)
    store_q = pltpu.make_async_copy(r["q"], gq, r["load_sem"].at[2])
    store_q.start()

    for copy in ly:
        copy.wait()
    loss[...] = (loss_y[0] + loss_y[1] + loss_y[2] + loss_y[3])[:1, :1] / token_total

    for copy in spread(0):
        copy.wait_recv()
    for copy in second:
        copy.wait_recv()
    for side in range(2):
        row0 = OWN_B if side else OWN_A
        acc = kv[row0 : row0 + HALF, :].astype(f32)
        for k in range(3):
            at = 384 * side + HALF * k
            acc = acc + r["got"][0, at : at + HALF, :].astype(f32)
        for k in range(3):
            acc = acc + r["got2"][side, k].astype(f32)
        kv[row0 : row0 + HALF, :] = acc.astype(bf16)
        half = slice(HALF, 2 * HALF) if side else slice(0, HALF)
        for n, (out, lanes) in enumerate(((gpk, slice(0, DH)), (gpv, slice(DH, 2 * DH)))):
            store = pltpu.make_async_copy(
                kv.at[row0 : row0 + HALF, lanes], out.at[half], r["load_sem"].at[3 + 2 * side + n]
            )
            store.start()
            stores.append(store)

    for store in stores:
        store.wait()
    store_q.wait()
    for i in range(4):
        for copy in spread(i):
            copy.wait_send()
    for copy in second:
        copy.wait_send()


def hand_over(*refs):
    for src, dst in zip(refs[:5], refs[5:]):
        dst[...] = src[...]


def on_device(query, resp_key, resp_value, prefix_key, prefix_value, readout, base, ref, adv, rlen, count):
    hbm = pl.BlockSpec(memory_space=pl.ANY)
    smem = pl.BlockSpec(memory_space=pltpu.SMEM)
    like = lambda x: jax.ShapeDtypeStruct(x.shape, bf16)
    flops = 5 * 2 * KEYS * ROWS * DH
    loss, gq, grk, grv, gpk, gpv = pl.pallas_call(
        kernel,
        out_shape=(
            jax.ShapeDtypeStruct((1, 1), f32),
            like(query),
            like(resp_key),
            like(resp_value),
            like(prefix_key),
            like(prefix_value),
        ),
        in_specs=[hbm] * 8 + [smem] * 3,
        out_specs=(pl.BlockSpec(memory_space=pltpu.VMEM),) + (hbm,) * 5,
        scratch_shapes=scratch(),
        cost_estimate=pl.CostEstimate(
            flops=flops, bytes_accessed=4 * 2**20, transcendentals=KEYS * ROWS
        ),
        compiler_params=pltpu.CompilerParams(
            collective_id=0, has_side_effects=True, vmem_limit_bytes=64 * 2**20 - 2**17
        ),
    )(
        query,
        readout,
        resp_key,
        resp_value,
        prefix_key,
        prefix_value,
        base.reshape(1, TOK),
        ref.reshape(1, TOK),
        adv,
        rlen,
        count,
    )
    grads = pl.pallas_call(
        hand_over,
        out_shape=tuple(like(x) for x in (gq, grk, grv, gpk, gpv)),
        in_specs=[pl.BlockSpec(memory_space=pltpu.VMEM)] * 5,
        out_specs=(pl.BlockSpec(memory_space=pltpu.VMEM),) * 5,
    )(gq, grk, grv, gpk, gpv)
    return (loss.reshape(1),) + tuple(grads)


def solution(mesh):
    both = P("group", "tensor")
    one = P("group")
    in_specs = (both,) * 6 + (one,) * 4 + (P(),)
    out_specs = (P(),) + (both,) * 5
    return jax.shard_map(
        on_device, mesh=mesh, in_specs=in_specs, out_specs=out_specs, check_vma=False
    )
```

```python
import functools

import jax
import jax.numpy as jnp
from jax import lax
from jax.experimental import pallas as pl
from jax.experimental.pallas import tpu as pltpu
from jax.sharding import PartitionSpec as P

MESH = pl.DeviceIdType.MESH
bf16 = jnp.bfloat16
f32 = jnp.float32
NT = (((1,), (1,)), ((), ()))

DH = 128
TOK = 256
HPD = 8
ROWS = TOK * HPD
KEYS = 4096 + TOK
SIDE = 4
HALF = 128
STEPS = (1, 3, 2)
OWN_A, OWN_B, NEAR, FAR = 256, 384, 512, 1280
OWN, GROUP = 512, 768
LAST = 6
SCORE_SCALE = DH**-0.5
TO_LOG2 = SCORE_SCALE * 1.4426950408889634
SCORE_FLOOR = -1e30
GRAD_FACTOR = 64.0 * 4096.0


def block_at(b):
    if isinstance(b, int):
        size = {0: OWN, 5: 512, 6: 256}.get(b, GROUP)
        return (0 if b == 0 else FAR + GROUP * 3 + 512 if b == 6 else OWN + GROUP * (b - 1)), size
    return pl.multiple_of(OWN + GROUP * (b - 1), 256), GROUP


def place(side, k):
    return 512 + HALF * side if k == 2 else 256 * side + HALF * k


def fold_rows(x):
    return jnp.sum(x.reshape(-1, 8, x.shape[-1]), 0)


def cols(h, width):
    return slice(h * width, (h + 1) * width)


def score_stage(r, h, b, buf, first):
    row0, size = block_at(b)
    s = (
        lax.dot_general(
            r["kv"][pl.ds(row0, size), :DH],
            r["q"][:, cols(h, DH)],
            NT,
            preferred_element_type=f32,
        )
        * TO_LOG2
    )
    if first:
        key_at = lax.broadcasted_iota(jnp.int32, (TOK, TOK), 0)
        query_at = lax.broadcasted_iota(jnp.int32, (TOK, TOK), 1)
        s = jnp.concatenate([jnp.where(key_at <= query_at, s[:TOK], SCORE_FLOOR), s[TOK:]], 0)
    buf[:size, :] = s
    top = jnp.ceil(jnp.max(jnp.max(s.reshape(-1, 8, TOK), 0), 0, keepdims=True))
    if not first:
        top = jnp.maximum(top, r["top"][b - 1, h : h + 1, :])
    r["top"][b, h : h + 1, :] = top


def weight_stage(r, h, b, buf, first):
    row0, size = block_at(b)
    at = cols(h, TOK)
    along = lax.dot_general(
        r["kv"][pl.ds(row0, size), DH:],
        r["ro"][:, cols(h, DH)],
        NT,
        preferred_element_type=f32,
    )
    top = r["top"][b, h : h + 1, :]
    e = jnp.exp2(buf[:size, :] - top)
    r["e"][pl.ds(row0, size), at] = e.astype(bf16)
    r["along"][pl.ds(row0, size), at] = along
    if first:
        r["l"][:, at] = fold_rows(e)
        r["dot"][:, at] = fold_rows(e * along)
    else:
        shrink = jnp.exp2(r["top"][b - 1, h : h + 1, :] - top)
        r["l"][:, at] = r["l"][:, at] * shrink + fold_rows(e)
        r["dot"][:, at] = r["dot"][:, at] * shrink + fold_rows(e * along)


def forward_block(r, b, first=False):
    bufs = (r["s0"], r["s1"])
    score_stage(r, 0, b, bufs[0], first)
    for h in range(HPD):
        if h + 1 < HPD:
            score_stage(r, h + 1, b, bufs[(h + 1) % 2], first)
        weight_stage(r, h, b, bufs[h % 2], first)


def query_block(r, b, first=False):
    row0, size = block_at(b)
    rows = pl.ds(row0, size)
    r["kt"][:, :size] = jnp.transpose(r["kv"][rows, :DH].astype(f32)).astype(bf16)
    for h in range(HPD):
        at = cols(h, TOK)
        x = r["e"][rows, at].astype(f32) * (r["along"][rows, at] - r["mean"][h : h + 1, :])
        r["along"][rows, at] = x
        d = jnp.dot(r["kt"][:, :size], x.astype(bf16), preferred_element_type=f32)
        d = d * jnp.exp2(r["top"][b, h : h + 1, :] - r["top"][LAST, h : h + 1, :])
        r["dq"][:, at] = d if first else r["dq"][:, at] + d


def factor_block(r, b):
    c = jnp.transpose(r["c"][...] * jnp.exp2(r["top"][b] - r["top"][LAST]))
    ck = c * SCORE_SCALE
    for h in range(HPD):
        at = cols(h, TOK)
        r["wv"][at, :] = (r["ro"][:, cols(h, DH)].astype(f32) * c[:, h : h + 1]).astype(bf16)
        r["wq"][at, :] = (r["q"][:, cols(h, DH)].astype(f32) * ck[:, h : h + 1]).astype(bf16)


def grads(r, row0, size):
    rows = slice(row0, row0 + size)
    r["kv"][rows, DH:] = jnp.dot(
        r["e"][rows, :], r["wv"][...], preferred_element_type=f32
    ).astype(bf16)
    r["kv"][rows, :DH] = jnp.dot(
        r["along"][rows, :].astype(bf16), r["wq"][...], preferred_element_type=f32
    ).astype(bf16)


def judge(logit, ref_rows, is_valid, advantage, token_total):
    logprob = jnp.minimum(logit, 0.0) - jnp.log1p(jnp.exp(-jnp.abs(logit)))
    gap = ref_rows - logprob
    ratio = jnp.exp(gap)
    terms = jnp.where(is_valid, ratio - gap - 1.0 - advantage * logprob, 0.0)
    d_logit = jnp.where(
        is_valid, (1.0 - ratio - advantage) * jax.nn.sigmoid(-logit), 0.0
    ) * (GRAD_FACTOR / token_total)
    return d_logit, terms


NAMES = (
    ["e", "along", "kv", "q", "ro", "s0", "s1", "kt", "dq", "wv", "wq", "top", "l", "dot"]
    + ["mean", "c", "got", "got2", "part", "loss_z", "loss_y", "lb", "rf", "load_sem"]
    + ["ag_send", "ag_recv", "part_send", "part_recv", "rs_send", "rs_recv"]
    + ["rs2_send", "rs2_recv", "lz_send", "lz_recv", "ly_send", "ly_recv"]
)


def scratch():
    vm, dma = pltpu.VMEM, pltpu.SemaphoreType.DMA
    return [
        vm((KEYS, ROWS), bf16),
        vm((KEYS, ROWS), f32),
        vm((KEYS, 2 * DH), bf16),
        vm((TOK, HPD * DH), bf16),
        vm((TOK, HPD * DH), bf16),
        vm((GROUP, TOK), f32),
        vm((GROUP, TOK), f32),
        vm((DH, GROUP), bf16),
        vm((DH, ROWS), f32),
        vm((ROWS, DH), bf16),
        vm((ROWS, DH), bf16),
        vm((LAST + 1, HPD, TOK), f32),
        vm((8, ROWS), f32),
        vm((8, ROWS), f32),
        vm((HPD, TOK), f32),
        vm((HPD, TOK), f32),
        vm((4, 2, 3, HALF, 2 * DH), bf16),
        vm((2, 3, HALF, 2 * DH), bf16),
        vm((8, 8, TOK), f32),
        vm((SIDE, 8, 128), f32),
        vm((SIDE, 8, 128), f32),
        vm((1, TOK), f32),
        vm((1, TOK), f32),
        dma((16,)),
        dma((30,)),
        dma((30,)),
        dma((8,)),
        dma((8,)),
        dma((24,)),
        dma((24,)),
        dma((6,)),
        dma((6,)),
        dma((3,)),
        dma((SIDE,)),
        dma((3,)),
        dma((SIDE,)),
    ]


def kernel(*refs):
    (q, ro, rk, rv, pk, pv, lb, rf, adv, rlen, count) = refs[:11]
    (loss, gq, grk, grv, gpk, gpv) = refs[11:17]
    r = dict(zip(NAMES, refs[17:]))
    kv = r["kv"]

    g, t = lax.axis_index("group"), lax.axis_index("tensor")
    y, z = g // SIDE, g % SIDE

    def along_z(step):
        return (y * SIDE + (z + step) % SIDE, t)

    def along_y(step):
        return (((y + step) % SIDE) * SIDE + z, t)

    def in_tensor(step):
        return (g, (t + step) % 8)

    moves = [
        (pk.at[:HALF], kv.at[OWN_A : OWN_A + HALF, :DH]),
        (pk.at[HALF:], kv.at[OWN_B : OWN_B + HALF, :DH]),
        (pv.at[:HALF], kv.at[OWN_A : OWN_A + HALF, DH:]),
        (pv.at[HALF:], kv.at[OWN_B : OWN_B + HALF, DH:]),
        (rk, kv.at[:TOK, :DH]),
        (rv, kv.at[:TOK, DH:]),
        (q, r["q"]),
        (ro, r["ro"]),
        (lb, r["lb"]),
        (rf, r["rf"]),
    ]
    loads = [
        pltpu.make_async_copy(src, dst, r["load_sem"].at[i]) for i, (src, dst) in enumerate(moves)
    ]
    barrier = pltpu.get_barrier_semaphore()
    peers = (
        [along_z(d) for d in STEPS]
        + [along_y(d) for d in STEPS]
        + [in_tensor(d) for d in range(1, 8)]
    )
    for peer in peers:
        pl.semaphore_signal(barrier, inc=1, device_id=peer, device_id_type=MESH)
    for load in loads:
        load.start()
    for load in loads[:4]:
        load.wait()
    pl.semaphore_wait(barrier, len(peers))

    def part_of_code(body):
        pl.when(t >= 0)(body)

    def remote(src, dst, send_sem, recv_sem, peer):
        return pltpu.make_async_remote_copy(
            src_ref=src,
            dst_ref=dst,
            send_sem=send_sem,
            recv_sem=recv_sem,
            device_id=peer,
            device_id_type=MESH,
        )

    def gather_copy(slot, src_row, dst_row, peer):
        return remote(
            kv.at[src_row : src_row + HALF],
            kv.at[dst_row : dst_row + HALF],
            r["ag_send"].at[slot],
            r["ag_recv"].at[slot],
            peer,
        )

    near = [gather_copy(j, OWN_A, NEAR + HALF * j, along_z(-STEPS[j])) for j in range(3)]
    near += [
        gather_copy(3 + j, OWN_B, NEAR + 384 + HALF * j, along_y(-STEPS[j])) for j in range(3)
    ]
    far = []
    for i in range(4):
        src_a = OWN_A if i == 0 else NEAR + HALF * (i - 1)
        src_b = OWN_B if i == 0 else NEAR + 384 + HALF * (i - 1)
        dst = FAR + GROUP * i
        far.append(
            [
                gather_copy(6 + 6 * i + k, src_a, dst + place(0, k), along_y(-STEPS[k]))
                for k in range(3)
            ]
            + [
                gather_copy(9 + 6 * i + k, src_b, dst + place(1, k), along_z(-STEPS[k]))
                for k in range(3)
            ]
        )
    for copy in near + far[0]:
        copy.start()
    for load in loads[4:]:
        load.wait()

    part_of_code(lambda: forward_block(r, 0, True))

    def forward_step(b, carry):
        @pl.when(b == 1)
        def _():
            for j in range(3):
                near[j].wait_recv()
                near[3 + j].wait_recv()
                for copy in far[j + 1]:
                    copy.start()

        for i in range(3):

            @pl.when(b == 2 + i)
            def _():
                for copy in far[i]:
                    copy.wait_recv()

        forward_block(r, b)
        return carry

    lax.fori_loop(1, 5, forward_step, 0)
    for n in (0, 1, 3, 4):
        far[3][n].wait_recv()
    part_of_code(lambda: forward_block(r, 5))
    for n in (2, 5):
        far[3][n].wait_recv()
    part_of_code(lambda: forward_block(r, 6))

    total = jnp.zeros((1, TOK), f32)
    sums = []
    for h in range(HPD):
        at = cols(h, TOK)
        row_sum = jnp.sum(r["l"][:, at], 0, keepdims=True)
        mean = jnp.sum(r["dot"][:, at], 0, keepdims=True) / row_sum
        r["mean"][h : h + 1, :] = mean
        r["c"][h : h + 1, :] = 1.0 / row_sum
        total = total + mean
    part = r["part"]
    part[t] = jnp.broadcast_to(total, (8, TOK))
    part_copies = [
        remote(
            part.at[t], part.at[t], r["part_send"].at[d], r["part_recv"].at[d], in_tensor(d)
        )
        for d in range(1, 8)
    ]
    for copy in part_copies:
        copy.start()

    for b in range(LAST + 1):
        part_of_code(functools.partial(query_block, r, b, b == 0))

    for copy in part_copies:
        copy.wait()
    logit = r["lb"][...]
    for i in range(8):
        logit = logit + part[i, 0:1, :]
    token_total = count[0].astype(f32)
    is_valid = lax.broadcasted_iota(jnp.int32, (1, TOK), 1) < rlen[0]
    d_logit, terms = judge(logit, r["rf"][...], is_valid, adv[0], token_total)
    r["c"][...] = r["c"][...] * d_logit

    loss_z, loss_y = r["loss_z"], r["loss_y"]
    loss_z[z] = jnp.broadcast_to(jnp.sum(terms, axis=1, keepdims=True), (8, 128))
    lz = [
        remote(
            loss_z.at[z], loss_z.at[z], r["lz_send"].at[j], r["lz_recv"].at[STEPS[j]], along_z(STEPS[j])
        )
        for j in range(3)
    ]
    for copy in lz:
        copy.start()

    for copy in near:
        copy.wait_send()
    for group in far:
        for copy in group:
            copy.wait_send()

    def axis_of(side, step):
        return along_z(step) if side else along_y(step)

    def spread(i, numbers=range(3)):
        return [
            remote(
                kv.at[pl.ds(FAR + GROUP * i + place(side, k), HALF)],
                r["got"].at[i, side, k],
                r["rs_send"].at[6 * i + 3 * side + k],
                r["rs_recv"].at[6 * i + 3 * side + k],
                axis_of(side, STEPS[k]),
            )
            for side in range(2)
            for k in numbers
        ]

    second = []

    def second_stage(i):
        for copy in spread(i):
            copy.wait_recv()
        for side in range(2):
            row0 = NEAR + 384 * side + HALF * (i - 1)
            acc = kv[row0 : row0 + HALF, :].astype(f32)
            for k in range(3):
                acc = acc + r["got"][i, side, k].astype(f32)
            kv[row0 : row0 + HALF, :] = acc.astype(bf16)
            slot = 2 * (i - 1) + side
            copy = remote(
                kv.at[row0 : row0 + HALF],
                r["got2"].at[side, i - 1],
                r["rs2_send"].at[slot],
                r["rs2_recv"].at[slot],
                axis_of(1 - side, STEPS[i - 1]),
            )
            copy.start()
            second.append(copy)

    def own_grads(b):
        def body():
            factor_block(r, b)
            grads(r, *block_at(b))

        part_of_code(body)

    def first_piece():
        factor_block(r, 3)
        grads(r, FAR + GROUP, 512)

    part_of_code(first_piece)
    for copy in spread(1, range(2)):
        copy.start()
    part_of_code(lambda: grads(r, FAR + GROUP + 512, 256))
    for copy in spread(1, range(2, 3)):
        copy.start()
    own_grads(4)
    for copy in spread(2):
        copy.start()

    for copy in lz:
        copy.wait()
    loss_y[y] = loss_z[0] + loss_z[1] + loss_z[2] + loss_z[3]
    ly = [
        remote(
            loss_y.at[y], loss_y.at[y], r["ly_send"].at[j], r["ly_recv"].at[STEPS[j]], along_y(STEPS[j])
        )
        for j in range(3)
    ]
    for copy in ly:
        copy.start()

    own_grads(5)
    for copy in spread(3, range(2)):
        copy.start()
    own_grads(6)
    for copy in spread(3, range(2, 3)):
        copy.start()
    own_grads(2)
    for copy in spread(0):
        copy.start()
    own_grads(1)
    second_stage(1)
    own_grads(0)
    stores = [
        pltpu.make_async_copy(kv.at[:TOK, :DH], grk, r["load_sem"].at[0]),
        pltpu.make_async_copy(kv.at[:TOK, DH:], grv, r["load_sem"].at[1]),
    ]
    for store in stores:
        store.start()
    second_stage(2)

    for h in range(HPD):
        d = r["dq"][:, cols(h, TOK)] * (r["c"][h : h + 1, :] * SCORE_SCALE)
        r["q"][:, cols(h, DH)] = jnp.transpose(d).astype(bf16)
    store_q = pltpu.make_async_copy(r["q"], gq, r["load_sem"].at[2])
    store_q.start()
    second_stage(3)

    for copy in ly:
        copy.wait()
    loss[...] = (loss_y[0] + loss_y[1] + loss_y[2] + loss_y[3])[:1, :1] / token_total

    for copy in spread(0):
        copy.wait_recv()
    for copy in second:
        copy.wait_recv()
    for side in range(2):
        row0 = OWN_B if side else OWN_A
        acc = kv[row0 : row0 + HALF, :].astype(f32)
        for k in range(3):
            acc = acc + r["got"][0, side, k].astype(f32)
        for k in range(3):
            acc = acc + r["got2"][side, k].astype(f32)
        kv[row0 : row0 + HALF, :] = acc.astype(bf16)
        half = slice(HALF, 2 * HALF) if side else slice(0, HALF)
        for n, (out, lanes) in enumerate(((gpk, slice(0, DH)), (gpv, slice(DH, 2 * DH)))):
            store = pltpu.make_async_copy(
                kv.at[row0 : row0 + HALF, lanes], out.at[half], r["load_sem"].at[3 + 2 * side + n]
            )
            store.start()
            stores.append(store)

    for store in stores:
        store.wait()
    store_q.wait()
    for i in range(4):
        for copy in spread(i):
            copy.wait_send()
    for copy in second:
        copy.wait_send()


def hand_over(*refs):
    srcs, dsts, held, sems = refs[:5], refs[5:10], refs[10:15], refs[15]
    pieces = [(0, slice(64 * n, 64 * n + 64)) for n in range(4)]
    pieces += [(n, slice(0, TOK)) for n in range(1, 5)]
    reads = [
        pltpu.make_async_copy(srcs[n].at[rows], held[n].at[rows], sems.at[0, at])
        for at, (n, rows) in enumerate(pieces)
    ]
    writes = [
        pltpu.make_async_copy(held[n].at[rows], dsts[n].at[rows], sems.at[1, at])
        for at, (n, rows) in enumerate(pieces)
    ]
    for read in reads:
        read.start()
    for read, write in zip(reads, writes):
        read.wait()
        write.start()
    for write in writes:
        write.wait()


def on_device(query, resp_key, resp_value, prefix_key, prefix_value, readout, base, ref, adv, rlen, count):
    hbm = pl.BlockSpec(memory_space=pl.ANY)
    smem = pl.BlockSpec(memory_space=pltpu.SMEM)
    like = lambda x: jax.ShapeDtypeStruct(x.shape, bf16)
    flops = 5 * 2 * KEYS * ROWS * DH
    loss, gq, grk, grv, gpk, gpv = pl.pallas_call(
        kernel,
        out_shape=(
            jax.ShapeDtypeStruct((1, 1), f32),
            like(query),
            like(resp_key),
            like(resp_value),
            like(prefix_key),
            like(prefix_value),
        ),
        in_specs=[hbm] * 8 + [smem] * 3,
        out_specs=(pl.BlockSpec(memory_space=pltpu.VMEM),) + (hbm,) * 5,
        scratch_shapes=scratch(),
        cost_estimate=pl.CostEstimate(
            flops=flops, bytes_accessed=4 * 2**20, transcendentals=KEYS * ROWS
        ),
        compiler_params=pltpu.CompilerParams(
            collective_id=0, has_side_effects=True, vmem_limit_bytes=64 * 2**20 - 2**17
        ),
    )(
        query,
        readout,
        resp_key,
        resp_value,
        prefix_key,
        prefix_value,
        base.reshape(1, TOK),
        ref.reshape(1, TOK),
        adv,
        rlen,
        count,
    )
    grads = pl.pallas_call(
        hand_over,
        out_shape=tuple(like(x) for x in (gq, grk, grv, gpk, gpv)),
        in_specs=[hbm] * 5,
        out_specs=(hbm,) * 5,
        scratch_shapes=[pltpu.VMEM(x.shape, bf16) for x in (gq, grk, grv, gpk, gpv)]
        + [pltpu.SemaphoreType.DMA((2, 8))],
    )(gq, grk, grv, gpk, gpv)
    return (loss.reshape(1),) + tuple(grads)


def solution(mesh):
    both = P("group", "tensor")
    one = P("group")
    in_specs = (both,) * 6 + (one,) * 4 + (P(),)
    out_specs = (P(),) + (both,) * 5
    return jax.shard_map(
        on_device, mesh=mesh, in_specs=in_specs, out_specs=out_specs, check_vma=False
    )
```
